32 devices in a mesh: groups: 2 (over x), expert: 16 (over z, y, core).
Axes of the slice: x: 2, y: 2, z: 4, core: 2. Of those that a mesh axis runs over, the one named last changes fastest.
Arguments:
- tokens: bfloat16 [4096, 4096], P(('groups', 'expert')), parts along dimension 0, may hold values from -6 to 6
- cotangent: bfloat16 [4096, 4096], P(('groups', 'expert')), parts along dimension 0, may hold values from -6 to 6
- gate_weight: bfloat16 [4096, 16384], P(None, 'expert'), may hold values from -0.09375 to 0.09375
- up_weight: bfloat16 [4096, 16384], P(None, 'expert'), may hold values from -0.09375 to 0.09375
- down_weight: bfloat16 [16384, 4096], P('expert'), may hold values from -0.0625 to 0.0625
- chosen: int32 [4, 64], P('groups'), parts along dimension 0, may hold values from 0 to 2047, as said below
- counts: int32 [4], P('groups'), parts along dimension 0, may hold values from 8 to 64, as said below
- gate_values: float32 [4, 64], P('groups'), parts along dimension 0, may hold values from 0.1 to 1
Outputs:
- layer_out: bfloat16 [4096, 4096], P(('groups', 'expert')), parts along dimension 0
- token_grad: bfloat16 [4096, 4096], P(('groups', 'expert')), parts along dimension 0
- gate_grad: float32 [4, 64], P('groups'), parts along dimension 0
The draws below stay inside these ranges and needn't reach their ends.
There are 2 independent parts, one for each index of `groups`. The reference program is written for one: setup_inputs(seed, part) draws one part's arguments, and reference() takes and returns one part's arrays. A program takes and returns all parts, laid end to end along the dimension named above; an argument that names none is the same for every part. Nothing has to cross between parts.
Inputs may be any that keep to these rules, and one draw needn't show every extreme that they name: `chosen`: in each of the 2 rows the first counts[e] entries are distinct token indices in increasing order; at most 8 of them lie among the 128 tokens of one device (indices j * 128 to (j + 1) * 128 - 1), and in every draw each expert takes exactly 8 from some device. Entries from counts[e] on are padding with arbitrary values. `counts`: in every draw some expert has all 64 slots valid.
All inputs are finite; a program needn't handle non-finite values.
Results may differ from the reference program's by a relative error of at most 0.0058.
Values may be sent and summed in bfloat16 or wider, within the bound.
A program may use at most 128 MiB of HBM per device.

```python
import jax
import jax.numpy as jnp

D = 4096
FF_WIN = 8192
EXP_FLY = 2
TOK_DEV = 128
TOKENS = 2048
CAP = 64
SLOT = 8


def route_table(key):
    devices = TOKENS // TOK_DEV
    pair_count = devices // 2
    key_list = jax.random.split(key, 6)
    first_half = jax.random.randint(key_list[0], (EXP_FLY, pair_count), 0, SLOT + 1)
    forced = jax.random.randint(key_list[1], (EXP_FLY, 1), 0, pair_count)
    pair_index = jnp.arange(pair_count)[None, :]
    first_half = jnp.where(pair_index == forced, SLOT, first_half)
    second_raw = jax.random.randint(key_list[2], (EXP_FLY, pair_count), 0, SLOT + 1)
    full_expert = jax.random.randint(key_list[3], (), 0, EXP_FLY)
    is_full = jnp.arange(EXP_FLY)[:, None] == full_expert
    second_half = jnp.where(is_full, SLOT - first_half, second_raw % (SLOT + 1 - first_half))
    per_device = jnp.stack([first_half, second_half], axis=-1).reshape(EXP_FLY, devices)
    totals = jnp.sum(per_device, axis=1).astype(jnp.int32)
    scores = jax.random.randint(key_list[4], (EXP_FLY, devices, TOK_DEV), 0, 1 << 20) * TOK_DEV
    scores = scores + jnp.arange(TOK_DEV)[None, None, :]
    ranking = jnp.argsort(jnp.argsort(scores, axis=-1), axis=-1)
    picked = (ranking < per_device[:, :, None]).reshape(EXP_FLY, TOKENS)
    places = jnp.cumsum(picked.astype(jnp.int32), axis=1) - 1
    places = jnp.where(picked, places, CAP)
    filler = jax.random.randint(key_list[5], (EXP_FLY, CAP), 0, TOKENS)
    rows_index = jnp.broadcast_to(jnp.arange(EXP_FLY)[:, None], (EXP_FLY, TOKENS))
    token_ids = jnp.broadcast_to(jnp.arange(TOKENS)[None, :], (EXP_FLY, TOKENS)).astype(filler.dtype)
    token_table = filler.at[rows_index, places].set(token_ids, mode='drop')
    return (token_table.astype(jnp.int32), totals)


def draw_chosen(key, part):
    token_table, totals = route_table(key)
    return token_table


def draw_counts(key, part):
    token_table, totals = route_table(key)
    return totals


def block_levels(key, extent, shards, smallest, top_value):
    def one(axis_at, shards_of):
        steps = jax.random.uniform(jax.random.fold_in(jax.random.fold_in(key, 6), axis_at), (shards_of,), jnp.float32, smallest / len(shards), top_value / len(shards))
        return jnp.repeat(jnp.exp(steps), extent[axis_at] // shards_of).reshape((-1,) + (1,) * (len(extent) - axis_at - 1))

    loudness = one(*shards[0])
    for cut in shards[1:]:
        loudness = loudness * one(*cut)
    return loudness


def scatter_about(rng, extent, scale, reach, pieces=(), held_as=jnp.bfloat16):
    entries = scale * jax.random.normal(rng, extent, jnp.float32)
    if pieces:
        entries = entries * block_levels(rng, extent, pieces, -0.22, 0.18)
    return jnp.clip(entries, -reach, reach).astype(held_as)


def setup_inputs(seed: int = 0, part: int = 0) -> dict:
    key_of = jax.random.split(jax.random.key(seed), 9)
    own_keys = jax.random.split(jax.random.fold_in(key_of[8], part), 9)
    return {
        "tokens": scatter_about(own_keys[0], (TOKENS, D), 1.0, 6.0, ((0, 16),)),
        "cotangent": scatter_about(own_keys[1], (TOKENS, D), 1.0, 6.0, ((0, 16),)),
        "gate_weight": scatter_about(key_of[2], (D, EXP_FLY * FF_WIN), D ** -0.5, 0.09375, ((1, 16),)),
        "up_weight": scatter_about(key_of[3], (D, EXP_FLY * FF_WIN), D ** -0.5, 0.09375, ((1, 16),)),
        "down_weight": scatter_about(key_of[4], (EXP_FLY * FF_WIN, D), FF_WIN ** -0.5, 0.0625, ((0, 16),)),
        "chosen": draw_chosen(jax.random.fold_in(jax.random.fold_in(key_of[8], part), 71), part),
        "counts": draw_counts(jax.random.fold_in(jax.random.fold_in(key_of[8], part), 71), part),
        "gate_values": jnp.clip(jax.random.uniform(own_keys[7], (EXP_FLY, CAP), jnp.float32, 0.1, 1.0), 0.1, 1.0),
    }


def reference(tokens, cotangent, gate_weight, up_weight, down_weight, chosen, counts, gate_values):
    mixed_sum = jnp.zeros((TOKENS, D), jnp.float32)
    grad_sum = jnp.zeros((TOKENS, D), jnp.float32)
    gate_rows = []
    for expert in range(EXP_FLY):
        lower_edge = expert * FF_WIN
        gate_block = gate_weight[:, lower_edge:lower_edge + FF_WIN]
        up_block = up_weight[:, lower_edge:lower_edge + FF_WIN]
        down_block = down_weight[lower_edge:lower_edge + FF_WIN, :]
        live_mask = jnp.arange(CAP) < counts[expert]
        index_row = chosen[expert].astype(jnp.int32)
        weight_row = jnp.where(live_mask, gate_values[expert], jnp.zeros_like(gate_values[expert]))
        expert_rows = tokens[index_row]
        expert_grads = cotangent[index_row]
        pre_gate = jnp.dot(expert_rows, gate_block, preferred_element_type=jnp.float32)
        pre_up = jnp.dot(expert_rows, up_block, preferred_element_type=jnp.float32)
        gate_sigmoid = jax.nn.sigmoid(pre_gate)
        activated = pre_gate * gate_sigmoid
        hidden = (activated * pre_up).astype(jnp.bfloat16)
        expert_out = jnp.dot(hidden, down_block, preferred_element_type=jnp.float32)
        mixed_sum = mixed_sum.at[index_row].add(weight_row[:, None] * expert_out)
        inner = jnp.sum(expert_out * expert_grads.astype(jnp.float32), axis=1)
        gate_rows.append(jnp.where(live_mask, inner, jnp.zeros_like(inner)))
        scaled = (weight_row[:, None] * expert_grads.astype(jnp.float32)).astype(jnp.bfloat16)
        back_hidden = jnp.dot(scaled, down_block.T, preferred_element_type=jnp.float32)
        grad_gate_in = (back_hidden * pre_up * gate_sigmoid * (1.0 + pre_gate * (1.0 - gate_sigmoid))).astype(jnp.bfloat16)
        grad_up_in = (back_hidden * activated).astype(jnp.bfloat16)
        input_grad = jnp.dot(grad_gate_in, gate_block.T, preferred_element_type=jnp.float32)
        input_grad = input_grad + jnp.dot(grad_up_in, up_block.T, preferred_element_type=jnp.float32)
        grad_sum = grad_sum.at[index_row].add(input_grad)
    return mixed_sum.astype(jnp.bfloat16), grad_sum.astype(jnp.bfloat16), jnp.stack(gate_rows)
```

```python
import functools

import jax
import jax.numpy as jnp
from jax import lax
from jax.experimental import pallas as pl
from jax.experimental.pallas import tpu as pltpu
from jax.sharding import PartitionSpec as P

SLOT = 8
PAIR = 2 * SLOT
FAR = 1e9
F32 = jnp.float32
BF16 = jnp.bfloat16


def dot(a, b):
    return jnp.dot(a, b, preferred_element_type=F32)


def dot_nt(a, b):
    return lax.dot_general(a, b, (((1,), (1,)), ((), ())), preferred_element_type=F32)


def iota(shape, axis):
    return lax.broadcasted_iota(jnp.int32, shape, axis)


def hot(mask):
    return jnp.where(mask, 1.0, 0.0).astype(F32)


def kernel(
    n, experts, packed,
    tok_hbm, cot_hbm, wg_hbm, wu_hbm, wd_hbm, chosen_ref, counts_ref, gate_ref,
    out_ref, grad_ref, gg_ref,
    tok_v, cot_v, wg_v, wu_v, wd_v, send_a, land_a, rows_t, rows_g, acc_g, acc_u, acc_b, gg_acc,
    rs_send_v, rs_send_g, rs_v, rs_g, own_send_v, own_send_g, own_v, own_g, gg_send, gg_land,
    loc_sem, wg_sem, wu_sem, wd_sem,
    a_ss, a_rs, bt_ss, bt_rs, bg_ss, bg_rs, rv_ss, rv_rs, rg_ss, rg_rs, ov_ss, ov_rs, og_ss, og_rs, q_ss, q_rs,
):
    gw = n // experts
    me = lax.axis_index("expert")
    my_e = me // gw
    my_c = me % gw
    base = my_e * gw
    tok = tok_v.shape[0]
    chunk = rows_t.shape[2]
    cap = rows_t.shape[1]
    capl = gg_send.shape[1]

    def other(i):
        return lax.rem(me + i, n)

    def back(i):
        return lax.rem(me + n - i, n)

    def ring(i):
        return lax.rem(my_c + i, gw)

    def ring_back(i):
        return lax.rem(my_c + gw - i, gw)

    def remote(src, dst, ss, rs, to):
        return pltpu.make_async_remote_copy(
            src_ref=src, dst_ref=dst, send_sem=ss, recv_sem=rs,
            device_id={"expert": to}, device_id_type=pl.DeviceIdType.MESH,
        )

    tok_copy = pltpu.make_async_copy(tok_hbm, tok_v, loc_sem.at[0])
    cot_copy = pltpu.make_async_copy(cot_hbm, cot_v, loc_sem.at[1])
    tok_copy.start()
    cot_copy.start()

    def wg_copy(c):
        at = pl.multiple_of(c * chunk, chunk)
        return pltpu.make_async_copy(wg_hbm.at[pl.ds(at, chunk), :], wg_v.at[c], wg_sem.at[c])

    def wu_copy(c):
        at = pl.multiple_of(c * chunk, chunk)
        return pltpu.make_async_copy(wu_hbm.at[pl.ds(at, chunk), :], wu_v.at[c], wu_sem.at[c])

    def wd_copy(c):
        at = pl.multiple_of(c * chunk, chunk)
        return pltpu.make_async_copy(wd_hbm.at[:, pl.ds(at, chunk)], wd_v.at[c], wd_sem.at[c])

    barrier = pltpu.get_barrier_semaphore()

    @pl.loop(1, n)
    def _(i):
        pl.semaphore_signal(barrier, inc=1, device_id={"expert": other(i)}, device_id_type=pl.DeviceIdType.MESH)

    @pl.loop(0, gw)
    def _(i):
        c = ring_back(i)
        wg_copy(c).start()
        wu_copy(c).start()

    @pl.loop(0, gw)
    def _(i):
        wd_copy(ring(i)).start()

    k_row = iota((1, cap), 1)
    eye = iota((cap, cap), 0) == iota((cap, cap), 1)

    def table(e):
        row = jnp.where(k_row < counts_ref[e], chosen_ref[pl.ds(e, 1), :].astype(F32), FAR)
        col = jnp.sum(jnp.where(eye, row, 0.0), axis=1, keepdims=True)
        return row, col

    first = (me * tok).astype(F32)
    span = float(tok)
    pick = jnp.zeros((experts * SLOT, tok), F32)
    spread = jnp.zeros((tok, experts * SLOT), F32)
    for e in range(experts):
        row, col = table(e)
        start = jnp.sum(hot(row < first), axis=1, keepdims=True)
        j_col = iota((experts * SLOT, cap), 0) - e * SLOT
        j_row = iota((cap, experts * SLOT), 1) - e * SLOT
        a = hot((iota((experts * SLOT, cap), 1).astype(F32) == start + j_col.astype(F32)) & (j_col >= 0) & (j_col < SLOT))
        at = hot((iota((cap, experts * SLOT), 0).astype(F32) == start + j_row.astype(F32)) & (j_row >= 0) & (j_row < SLOT))
        b = hot(col == first + iota((cap, tok), 1).astype(F32))
        bt = hot(row == first + iota((tok, cap), 0).astype(F32))
        pick = pick + dot(a.astype(BF16), b.astype(BF16))
        spread = spread + dot(bt.astype(BF16), at.astype(BF16))
    pick = pick.astype(BF16)
    spread = spread.astype(BF16)

    row, col = table(my_e)
    j = iota((cap, n * PAIR), 1)
    dev = (j // PAIR).astype(F32) * span
    slot = j % PAIR
    start = jnp.sum(hot(col < dev), axis=0, keepdims=True)
    inside = col < dev + span
    k_col = iota((cap, n * PAIR), 0).astype(F32)
    from_t = hot(inside & (slot < SLOT) & (k_col == start + slot.astype(F32))).astype(BF16)
    from_g = hot(inside & (slot >= SLOT) & (k_col == start + (slot - SLOT).astype(F32))).astype(BF16)
    j8 = iota((n * SLOT, cap), 0)
    dev8 = (j8 // SLOT).astype(F32) * span
    start8 = jnp.sum(hot(row < dev8), axis=1, keepdims=True)
    to_slot = hot(
        (row < dev8 + span) & (iota((n * SLOT, cap), 1).astype(F32) == start8 + (j8 % SLOT).astype(F32))
    ).astype(BF16)
    weight_row = jnp.where(k_row < counts_ref[my_e], gate_ref[pl.ds(my_e, 1), :], 0.0)
    weight = jnp.sum(jnp.where(eye, weight_row, 0.0), axis=1, keepdims=True)
    live_row = k_row < counts_ref[my_e]
    live = jnp.sum(jnp.where(eye, hot(live_row), 0.0), axis=1, keepdims=True)

    tok_copy.wait()
    cot_copy.wait()

    @pl.loop(0, gw)
    def _(c):
        cols = pl.ds(pl.multiple_of(c * chunk, chunk), chunk)
        t = dot(pick, tok_v[:, cols])
        g = dot(pick, cot_v[:, cols])
        for e in range(experts):
            lo = e * SLOT
            send_a[e * gw + c] = jnp.concatenate([t[lo:lo + SLOT], g[lo:lo + SLOT]], axis=0).astype(BF16)

    pl.semaphore_wait(barrier, n - 1)

    def a_copy(to, slot_of):
        return remote(send_a.at[to], land_a.at[slot_of], a_ss.at[to], a_rs.at[slot_of], to)

    @pl.loop(1, n)
    def _(i):
        a_copy(other(i), me).start()

    land_a[me] = send_a[me]

    @pl.loop(1, n)
    def _(i):
        a_copy(me, back(i)).wait_recv()

    arrived = land_a[...].reshape(n * PAIR, chunk)
    rows_t[my_c] = dot(from_t, arrived).astype(BF16)

    def bt_copy(to, at):
        return remote(rows_t.at[at], rows_t.at[at], bt_ss.at[to], bt_rs.at[at], base + to)

    def bg_copy(to, at):
        return remote(rows_g.at[at], rows_g.at[at], bg_ss.at[to], bg_rs.at[at], base + to)

    @pl.loop(1, gw)
    def _(i):
        bt_copy(ring(i), my_c).start()

    rows_g[my_c] = dot(from_g, arrived).astype(BF16)

    @pl.loop(1, gw)
    def _(i):
        bg_copy(ring(i), my_c).start()

    wg_copy(my_c).wait()
    wu_copy(my_c).wait()
    acc_g[...] = dot(rows_t[my_c], wg_v[my_c])
    acc_u[...] = dot(rows_t[my_c], wu_v[my_c])

    @pl.loop(1, gw)
    def _(i):
        c = ring_back(i)
        bt_copy(my_c, c).wait_recv()
        wg_copy(c).wait()
        wu_copy(c).wait()
        x = rows_t[c]
        acc_g[...] += dot(x, wg_v[c])
        acc_u[...] += dot(x, wu_v[c])

    pre_gate = acc_g[...]
    hidden = (pre_gate * jax.nn.sigmoid(pre_gate) * acc_u[...]).astype(BF16)

    def rv_copy(to, at):
        return remote(rs_send_v.at[to], rs_v.at[at], rv_ss.at[to], rv_rs.at[at], base + to)

    def rg_copy(to, at):
        return remote(rs_send_g.at[to], rs_g.at[at], rg_ss.at[to], rg_rs.at[at], base + to)

    gg_acc[...] = jnp.zeros_like(gg_acc)

    @pl.loop(1, gw)
    def _(i):
        c = ring(i)
        bg_copy(my_c, c).wait_recv()
        wd_copy(c).wait()
        value = dot(hidden, wd_v[c])
        rs_send_v[c] = value.astype(BF16)
        rv_copy(c, my_c).start()
        gg_acc[...] += value * rows_g[c].astype(F32)

    wd_copy(my_c).wait()
    value = dot(hidden, wd_v[my_c])
    rs_v[my_c] = value.astype(BF16)
    terms = live * jnp.sum(gg_acc[...] + value * rows_g[my_c].astype(F32), axis=1, keepdims=True)
    wide = iota((cap, capl), 0) == iota((cap, capl), 1)
    gg_send[...] = jnp.broadcast_to(jnp.sum(jnp.where(wide, terms, 0.0), axis=0, keepdims=True), gg_send.shape)

    def q_copy(to, at):
        return remote(gg_send, gg_land.at[at], q_ss.at[to], q_rs.at[at], to)

    @pl.loop(1, n)
    def _(i):
        q_copy(other(i), me).start()

    gg_land[me] = gg_send[...]

    acc_b[...] = jnp.zeros_like(acc_b)

    @pl.loop(0, gw)
    def _(c):
        scaled = (weight * rows_g[c].astype(F32)).astype(BF16)
        acc_b[...] += dot_nt(scaled, wd_v[c])

    up = acc_u[...]
    sig = jax.nn.sigmoid(pre_gate)
    backed = acc_b[...]
    d_gate = (backed * up * sig * (1.0 + pre_gate * (1.0 - sig))).astype(BF16)
    d_up = (backed * (pre_gate * sig)).astype(BF16)

    def to_owners(term, buf):
        slots = dot(to_slot, term.astype(BF16)).reshape(n, SLOT, chunk)
        if packed:
            half = chunk // 2
            slots = jnp.concatenate([slots[:, :, :half], slots[:, :, half:]], axis=1).astype(BF16)
        buf[...] = slots

    def summed(buf):
        return lax.fori_loop(1, gw, lambda c, s: s + buf[c].astype(F32), buf[0].astype(F32))

    def ov_copy(to, at):
        return remote(own_send_v.at[to], own_v.at[at], ov_ss.at[to], ov_rs.at[at], to)

    def og_copy(to, at):
        return remote(own_send_g.at[to], own_g.at[at], og_ss.at[to], og_rs.at[at], to)

    @pl.loop(1, gw)
    def _(i):
        rv_copy(my_c, ring_back(i)).wait_recv()

    to_owners(weight * summed(rs_v), own_send_v)

    @pl.loop(1, n)
    def _(i):
        ov_copy(other(i), me).start()

    own_v[me] = own_send_v[me]

    @pl.loop(1, gw)
    def _(i):
        c = ring(i)
        rs_send_g[c] = (dot_nt(d_gate, wg_v[c]) + dot_nt(d_up, wu_v[c])).astype(BF16)
        rg_copy(c, my_c).start()

    rs_g[my_c] = (dot_nt(d_gate, wg_v[my_c]) + dot_nt(d_up, wu_v[my_c])).astype(BF16)

    @pl.loop(1, gw)
    def _(i):
        rg_copy(my_c, ring_back(i)).wait_recv()

    to_owners(summed(rs_g), own_send_g)

    @pl.loop(1, n)
    def _(i):
        og_copy(other(i), me).start()

    own_g[me] = own_send_g[me]

    def unpack(x):
        x = x.astype(F32)
        if packed:
            x = jnp.concatenate([x[:SLOT], x[SLOT:]], axis=1)
        return x

    def finish(buf, ref):
        @pl.loop(0, gw)
        def _(c):
            rows = jnp.concatenate([unpack(buf[e * gw + c]) for e in range(experts)], axis=0)
            cols = pl.ds(pl.multiple_of(c * chunk, chunk), chunk)
            ref[:, cols] = dot(spread, rows.astype(BF16)).astype(BF16)

    @pl.loop(1, n)
    def _(i):
        ov_copy(me, back(i)).wait_recv()

    finish(own_v, out_ref)

    @pl.loop(1, n)
    def _(i):
        q_copy(me, back(i)).wait_recv()

    for e in range(experts):
        total = lax.fori_loop(1, gw, lambda c, s: s + gg_land[e * gw + c], gg_land[e * gw])
        gg_ref[e:e + 1, :] = total[0:1, :cap]

    @pl.loop(1, n)
    def _(i):
        og_copy(me, back(i)).wait_recv()

    finish(own_g, grad_ref)

    @pl.loop(1, n)
    def _(i):
        to = other(i)
        a_copy(to, me).wait_send()
        q_copy(to, me).wait_send()
        ov_copy(to, me).wait_send()
        og_copy(to, me).wait_send()

    @pl.loop(1, gw)
    def _(i):
        to = ring(i)
        bt_copy(to, my_c).wait_send()
        bg_copy(to, my_c).wait_send()
        rv_copy(to, my_c).wait_send()
        rg_copy(to, my_c).wait_send()


def shards(tokens, cotangent, gate_weight, up_weight, down_weight, chosen, counts, gate_values):
    n = lax.axis_size("expert")
    experts, cap = chosen.shape
    gw = n // experts
    tok, d = tokens.shape
    ff = gate_weight.shape[1]
    chunk = d // gw
    capl = -(-cap // 128) * 128
    packed = chunk % 256 == 0
    own_shape = (n, PAIR, chunk // 2) if packed else (n, SLOT, chunk)
    own_type = BF16 if packed else F32
    vmem = pl.BlockSpec(memory_space=pltpu.VMEM)
    hbm = pl.BlockSpec(memory_space=pl.ANY)
    dma = pltpu.SemaphoreType.DMA
    return pl.pallas_call(
        functools.partial(kernel, n, experts, packed),
        out_shape=(
            jax.ShapeDtypeStruct((tok, d), BF16),
            jax.ShapeDtypeStruct((tok, d), BF16),
            jax.ShapeDtypeStruct((experts, cap), F32),
        ),
        in_specs=[hbm] * 5 + [vmem, pl.BlockSpec(memory_space=pltpu.SMEM), vmem],
        out_specs=(vmem, vmem, vmem),
        scratch_shapes=[
            pltpu.VMEM((tok, d), BF16),
            pltpu.VMEM((tok, d), BF16),
            pltpu.VMEM((gw, chunk, ff), BF16),
            pltpu.VMEM((gw, chunk, ff), BF16),
            pltpu.VMEM((gw, ff, chunk), BF16),
            pltpu.VMEM((n, PAIR, chunk), BF16),
            pltpu.VMEM((n, PAIR, chunk), BF16),
            pltpu.VMEM((gw, cap, chunk), BF16),
            pltpu.VMEM((gw, cap, chunk), BF16),
            pltpu.VMEM((cap, ff), F32),
            pltpu.VMEM((cap, ff), F32),
            pltpu.VMEM((cap, ff), F32),
            pltpu.VMEM((cap, chunk), F32),
            pltpu.VMEM((gw, cap, chunk), BF16),
            pltpu.VMEM((gw, cap, chunk), BF16),
            pltpu.VMEM((gw, cap, chunk), BF16),
            pltpu.VMEM((gw, cap, chunk), BF16),
            pltpu.VMEM(own_shape, own_type),
            pltpu.VMEM(own_shape, own_type),
            pltpu.VMEM(own_shape, own_type),
            pltpu.VMEM(own_shape, own_type),
            pltpu.VMEM((8, capl), F32),
            pltpu.VMEM((n, 8, capl), F32),
            dma((2,)), dma((gw,)), dma((gw,)), dma((gw,)),
            dma((n,)), dma((n,)),
            dma((gw,)), dma((gw,)), dma((gw,)), dma((gw,)),
            dma((gw,)), dma((gw,)), dma((gw,)), dma((gw,)),
            dma((n,)), dma((n,)), dma((n,)), dma((n,)), dma((n,)), dma((n,)),
        ],
        compiler_params=pltpu.CompilerParams(
            collective_id=0, has_side_effects=True, vmem_limit_bytes=56 * 1024 * 1024
        ),
        name="expert_layer",
    )(tokens, cotangent, gate_weight, up_weight, down_weight, chosen, counts, gate_values)


def solution(mesh):
    placed = (
        P(("groups", "expert"), None),
        P(("groups", "expert"), None),
        P(None, "expert"),
        P(None, "expert"),
        P("expert", None),
        P("groups", None),
        P("groups"),
        P("groups", None),
    )
    return jax.shard_map(
        shards,
        mesh=mesh,
        in_specs=placed,
        out_specs=(P(("groups", "expert"), None), P(("groups", "expert"), None), P("groups", None)),
        check_vma=False,
    )
```

```python
import functools

import jax
import jax.numpy as jnp
from jax import lax
from jax.experimental import pallas as pl
from jax.experimental.pallas import tpu as pltpu
from jax.sharding import PartitionSpec as P

SLOT = 8
PAIR = 2 * SLOT
FAR = 1e9
F32 = jnp.float32
BF16 = jnp.bfloat16


def dot(a, b):
    return jnp.dot(a, b, preferred_element_type=F32)


def dot_nt(a, b):
    return lax.dot_general(a, b, (((1,), (1,)), ((), ())), preferred_element_type=F32)


def iota(shape, axis):
    return lax.broadcasted_iota(jnp.int32, shape, axis)


def hot(mask):
    return jnp.where(mask, 1.0, 0.0).astype(F32)


def kernel(
    n, experts, packed,
    tok_hbm, cot_hbm, wg_hbm, wu_hbm, wd_hbm, chosen_ref, counts_ref, gate_ref,
    out_ref, grad_ref, spread_ref, gg_ref,
    tok_v, cot_v, wg_v, wu_v, wd_v, send_a, land_a, rows_t, rows_g, acc_g, acc_u, acc_b, gg_acc,
    rs_send_v, rs_send_g, sib_v, sib_g, rs_v, rs_g, own_send_v, own_send_g, own_v, own_g, gg_send, gg_land,
    loc_sem, wg_sem, wu_sem, wd_sem,
    a_ss, a_rs, bt_ss, bt_rs, bg_ss, bg_rs, rv_ss, sv_rs, rv_rs, rg_ss, sg_rs, rg_rs, ov_ss, ov_rs, og_ss, og_rs, q_ss, q_rs,
):
    gw = n // experts
    me = lax.axis_index("expert")
    my_e = me // gw
    my_c = me % gw
    chips = gw // 2
    my_chip = my_c // 2
    core = my_c % 2
    sib = my_chip * 2 + 1 - core
    base = my_e * gw
    tok = tok_v.shape[0]
    chunk = rows_t.shape[2]
    cap = rows_t.shape[1]
    capl = gg_send.shape[1]

    def other(i):
        return lax.rem(me + i, n)

    def back(i):
        return lax.rem(me + n - i, n)

    def ring(i):
        return lax.rem(my_c + i, gw)

    def ring_back(i):
        return lax.rem(my_c + gw - i, gw)

    def near(i):
        return lax.rem(my_chip + i, chips) * 2 + core

    def near_back(i):
        return lax.rem(my_chip + chips - i, chips) * 2 + core

    def twin(c):
        return c + 1 - 2 * core

    def remote(src, dst, ss, rs, to):
        return pltpu.make_async_remote_copy(
            src_ref=src, dst_ref=dst, send_sem=ss, recv_sem=rs,
            device_id={"expert": to}, device_id_type=pl.DeviceIdType.MESH,
        )

    tok_copy = pltpu.make_async_copy(tok_hbm, tok_v, loc_sem.at[0])
    cot_copy = pltpu.make_async_copy(cot_hbm, cot_v, loc_sem.at[1])
    tok_copy.start()
    cot_copy.start()

    def wg_copy(c):
        at = pl.multiple_of(c * chunk, chunk)
        return pltpu.make_async_copy(wg_hbm.at[pl.ds(at, chunk), :], wg_v.at[c], wg_sem.at[c])

    def wu_copy(c):
        at = pl.multiple_of(c * chunk, chunk)
        return pltpu.make_async_copy(wu_hbm.at[pl.ds(at, chunk), :], wu_v.at[c], wu_sem.at[c])

    def wd_copy(c):
        at = pl.multiple_of(c * chunk, chunk)
        return pltpu.make_async_copy(wd_hbm.at[:, pl.ds(at, chunk)], wd_v.at[c], wd_sem.at[c])

    barrier = pltpu.get_barrier_semaphore()

    @pl.loop(1, n)
    def _(i):
        pl.semaphore_signal(barrier, inc=1, device_id={"expert": other(i)}, device_id_type=pl.DeviceIdType.MESH)

    @pl.loop(0, gw)
    def _(i):
        c = ring_back(i)
        wg_copy(c).start()
        wu_copy(c).start()

    @pl.loop(0, gw)
    def _(i):
        wd_copy(ring(i)).start()

    k_row = iota((1, cap), 1)
    eye = iota((cap, cap), 0) == iota((cap, cap), 1)

    def table(e):
        row = jnp.where(k_row < counts_ref[e], chosen_ref[pl.ds(e, 1), :].astype(F32), FAR)
        col = jnp.sum(jnp.where(eye, row, 0.0), axis=1, keepdims=True)
        return row, col

    first = (me * tok).astype(F32)
    span = float(tok)
    pick = jnp.zeros((experts * SLOT, tok), F32)
    for e in range(experts):
        row, col = table(e)
        start = jnp.sum(hot(row < first), axis=1, keepdims=True)
        j_col = iota((experts * SLOT, cap), 0) - e * SLOT
        a = hot((iota((experts * SLOT, cap), 1).astype(F32) == start + j_col.astype(F32)) & (j_col >= 0) & (j_col < SLOT))
        b = hot(col == first + iota((cap, tok), 1).astype(F32))
        pick = pick + dot(a.astype(BF16), b.astype(BF16))
    pick = pick.astype(BF16)

    tok_copy.wait()
    cot_copy.wait()

    @pl.loop(0, gw)
    def _(c):
        cols = pl.ds(pl.multiple_of(c * chunk, chunk), chunk)
        t = dot(pick, tok_v[:, cols])
        g = dot(pick, cot_v[:, cols])
        for e in range(experts):
            lo = e * SLOT
            send_a[e * gw + c] = jnp.concatenate([t[lo:lo + SLOT], g[lo:lo + SLOT]], axis=0).astype(BF16)

    pl.semaphore_wait(barrier, n - 1)

    def a_copy(to, slot_of):
        return remote(send_a.at[to], land_a.at[slot_of], a_ss.at[to], a_rs.at[slot_of], to)

    @pl.loop(1, n)
    def _(i):
        a_copy(other(i), me).start()

    land_a[me] = send_a[me]

    row, col = table(my_e)
    j = iota((cap, n * PAIR), 1)
    dev = (j // PAIR).astype(F32) * span
    slot = j % PAIR
    start = jnp.sum(hot(col < dev), axis=0, keepdims=True)
    inside = col < dev + span
    k_col = iota((cap, n * PAIR), 0).astype(F32)
    from_t = hot(inside & (slot < SLOT) & (k_col == start + slot.astype(F32))).astype(BF16)
    from_g = hot(inside & (slot >= SLOT) & (k_col == start + (slot - SLOT).astype(F32))).astype(BF16)
    j8 = iota((n * SLOT, cap), 0)
    dev8 = (j8 // SLOT).astype(F32) * span
    start8 = jnp.sum(hot(row < dev8), axis=1, keepdims=True)
    to_slot = hot(
        (row < dev8 + span) & (iota((n * SLOT, cap), 1).astype(F32) == start8 + (j8 % SLOT).astype(F32))
    ).astype(BF16)
    weight_row = jnp.where(k_row < counts_ref[my_e], gate_ref[pl.ds(my_e, 1), :], 0.0)
    weight = jnp.sum(jnp.where(eye, weight_row, 0.0), axis=1, keepdims=True)
    live_row = k_row < counts_ref[my_e]
    live = jnp.sum(jnp.where(eye, hot(live_row), 0.0), axis=1, keepdims=True)
    spread = jnp.zeros((tok, experts * SLOT), F32)
    for e in range(experts):
        row, _ = table(e)
        start = jnp.sum(hot(row < first), axis=1, keepdims=True)
        j_row = iota((cap, experts * SLOT), 1) - e * SLOT
        at = hot((iota((cap, experts * SLOT), 0).astype(F32) == start + j_row.astype(F32)) & (j_row >= 0) & (j_row < SLOT))
        bt = hot(row == first + iota((tok, cap), 0).astype(F32))
        spread = spread + dot(bt.astype(BF16), at.astype(BF16))
    spread_ref[...] = spread.astype(BF16)

    @pl.loop(1, n)
    def _(i):
        a_copy(me, back(i)).wait_recv()

    arrived = land_a[...].reshape(n * PAIR, chunk)
    rows_t[my_c] = dot(from_t, arrived).astype(BF16)

    def bt_copy(to, at, sem):
        return remote(rows_t.at[at], rows_t.at[at], bt_ss.at[sem], bt_rs.at[at], base + to)

    def bg_copy(to, at, sem):
        return remote(rows_g.at[at], rows_g.at[at], bg_ss.at[sem], bg_rs.at[at], base + to)

    @pl.loop(1, chips)
    def _(i):
        c = near(i)
        bt_copy(c, my_c, c).start()

    bt_copy(sib, my_c, sib).start()
    rows_g[my_c] = dot(from_g, arrived).astype(BF16)

    @pl.loop(1, chips)
    def _(i):
        c = near(i)
        bg_copy(c, my_c, c).start()

    bg_copy(sib, my_c, sib).start()

    def gate_up(c):
        wg_copy(c).wait()
        wu_copy(c).wait()
        x = rows_t[c]
        acc_g[...] += dot(x, wg_v[c])
        acc_u[...] += dot(x, wu_v[c])

    acc_g[...] = jnp.zeros_like(acc_g)
    acc_u[...] = jnp.zeros_like(acc_u)
    gate_up(my_c)
    bt_copy(my_c, sib, sib).wait_recv()
    gate_up(sib)

    @pl.loop(1, chips)
    def _(i):
        c = near_back(i)
        bt_copy(my_c, c, c).wait_recv()
        bt_copy(sib, c, twin(c)).start()
        gate_up(c)

    @pl.loop(1, chips)
    def _(i):
        c = near_back(i)
        bg_copy(my_c, c, c).wait_recv()
        bg_copy(sib, c, twin(c)).start()
        bt_copy(my_c, twin(c), c).wait_recv()
        gate_up(twin(c))

    pre_gate = acc_g[...]
    hidden = (pre_gate * jax.nn.sigmoid(pre_gate) * acc_u[...]).astype(BF16)

    def sv_copy(c, at):
        return remote(rs_send_v.at[c], sib_v.at[at], rv_ss.at[c], sv_rs.at[at], base + sib)

    def rv_copy(to, at):
        return remote(rs_send_v.at[to], rs_v.at[at], rv_ss.at[to], rv_rs.at[at], base + to)

    def sg_copy(c, at):
        return remote(rs_send_g.at[c], sib_g.at[at], rg_ss.at[c], sg_rs.at[at], base + sib)

    def rg_copy(to, at):
        return remote(rs_send_g.at[to], rs_g.at[at], rg_ss.at[to], rg_rs.at[at], base + to)

    gg_acc[...] = jnp.zeros_like(gg_acc)

    @pl.loop(1, chips + 1)
    def _(i):
        c = twin(near(i))
        bg_copy(my_c, c, c).wait_recv()
        wd_copy(c).wait()
        value = dot(hidden, wd_v[c])
        rs_send_v[c] = value.astype(BF16)
        sv_copy(c, c // 2).start()
        gg_acc[...] += value * rows_g[c].astype(F32)

    @pl.loop(1, chips)
    def _(i):
        c = near(i)
        wd_copy(c).wait()
        value = dot(hidden, wd_v[c])
        gg_acc[...] += value * rows_g[c].astype(F32)
        sv_copy(c, c // 2).wait_recv()
        rs_send_v[c] = (value + sib_v[c // 2].astype(F32)).astype(BF16)
        rv_copy(c, my_chip).start()

    wd_copy(my_c).wait()
    value = dot(hidden, wd_v[my_c])
    sv_copy(my_c, my_chip).wait_recv()
    rs_v[my_chip] = (value + sib_v[my_chip].astype(F32)).astype(BF16)
    terms = live * jnp.sum(gg_acc[...] + value * rows_g[my_c].astype(F32), axis=1, keepdims=True)
    wide = iota((cap, capl), 0) == iota((cap, capl), 1)
    gg_send[...] = jnp.broadcast_to(jnp.sum(jnp.where(wide, terms, 0.0), axis=0, keepdims=True), gg_send.shape)

    def q_copy(to, at):
        return remote(gg_send, gg_land.at[at], q_ss.at[to], q_rs.at[at], to)

    @pl.loop(1, n)
    def _(i):
        q_copy(other(i), me).start()

    gg_land[me] = gg_send[...]

    acc_b[...] = jnp.zeros_like(acc_b)

    @pl.loop(0, gw)
    def _(c):
        scaled = (weight * rows_g[c].astype(F32)).astype(BF16)
        acc_b[...] += dot_nt(scaled, wd_v[c])

    up = acc_u[...]
    sig = jax.nn.sigmoid(pre_gate)
    backed = acc_b[...]
    d_gate = (backed * up * sig * (1.0 + pre_gate * (1.0 - sig))).astype(BF16)
    d_up = (backed * (pre_gate * sig)).astype(BF16)

    def to_owners(term, buf):
        slots = dot(to_slot, term.astype(BF16)).reshape(n, SLOT, chunk)
        if packed:
            half = chunk // 2
            slots = jnp.concatenate([slots[:, :, :half], slots[:, :, half:]], axis=1).astype(BF16)
        buf[...] = slots

    def summed(buf):
        return lax.fori_loop(1, chips, lambda c, s: s + buf[c].astype(F32), buf[0].astype(F32))

    def ov_copy(to, at):
        return remote(own_send_v.at[to], own_v.at[at], ov_ss.at[to], ov_rs.at[at], to)

    def og_copy(to, at):
        return remote(own_send_g.at[to], own_g.at[at], og_ss.at[to], og_rs.at[at], to)

    @pl.loop(1, chips)
    def _(i):
        rv_copy(my_c, near_back(i) // 2).wait_recv()

    to_owners(weight * summed(rs_v), own_send_v)

    @pl.loop(1, n)
    def _(i):
        ov_copy(other(i), me).start()

    own_v[me] = own_send_v[me]

    def token_part(c):
        return dot_nt(d_gate, wg_v[c]) + dot_nt(d_up, wu_v[c])

    @pl.loop(1, chips + 1)
    def _(i):
        c = twin(near(i))
        rs_send_g[c] = token_part(c).astype(BF16)
        sg_copy(c, c // 2).start()

    @pl.loop(1, chips)
    def _(i):
        c = near(i)
        part = token_part(c)
        sg_copy(c, c // 2).wait_recv()
        rs_send_g[c] = (part + sib_g[c // 2].astype(F32)).astype(BF16)
        rg_copy(c, my_chip).start()

    part = token_part(my_c)
    sg_copy(my_c, my_chip).wait_recv()
    rs_g[my_chip] = (part + sib_g[my_chip].astype(F32)).astype(BF16)

    @pl.loop(1, chips)
    def _(i):
        rg_copy(my_c, near_back(i) // 2).wait_recv()

    to_owners(summed(rs_g), own_send_g)

    @pl.loop(1, n)
    def _(i):
        og_copy(other(i), me).start()

    own_g[me] = own_send_g[me]

    def unpack(x):
        x = x.astype(F32)
        if packed:
            x = jnp.concatenate([x[:SLOT], x[SLOT:]], axis=1)
        return x

    def finish(buf, ref):
        @pl.loop(0, gw)
        def _(c):
            rows = jnp.concatenate([unpack(buf[e * gw + c]) for e in range(experts)], axis=0)
            cols = pl.ds(pl.multiple_of(c * chunk, chunk), chunk)
            ref[:, cols] = rows.astype(BF16)

    @pl.loop(1, n)
    def _(i):
        ov_copy(me, back(i)).wait_recv()

    finish(own_v, out_ref)

    @pl.loop(1, n)
    def _(i):
        q_copy(me, back(i)).wait_recv()

    for e in range(experts):
        total = lax.fori_loop(1, gw, lambda c, s: s + gg_land[e * gw + c], gg_land[e * gw])
        gg_ref[e:e + 1, :] = total[0:1, :cap]

    @pl.loop(1, n)
    def _(i):
        og_copy(me, back(i)).wait_recv()

    finish(own_g, grad_ref)

    @pl.loop(1, n)
    def _(i):
        to = other(i)
        a_copy(to, me).wait_send()
        q_copy(to, me).wait_send()
        ov_copy(to, me).wait_send()
        og_copy(to, me).wait_send()

    @pl.loop(1, gw)
    def _(i):
        c = ring(i)
        bt_copy(c, my_c, c).wait_send()
        bg_copy(c, my_c, c).wait_send()
        rv_copy(c, my_chip).wait_send()
        rg_copy(c, my_chip).wait_send()


def expand(spread_ref, value_ref, grad_ref, gg_in, out_ref, tg_ref, gg_ref):
    spread = spread_ref[...]
    out_ref[...] = dot(spread, value_ref[...]).astype(BF16)
    tg_ref[...] = dot(spread, grad_ref[...]).astype(BF16)
    gg_ref[...] = gg_in[...]


def shards(tokens, cotangent, gate_weight, up_weight, down_weight, chosen, counts, gate_values):
    n = lax.axis_size("expert")
    experts, cap = chosen.shape
    gw = n // experts
    tok, d = tokens.shape
    ff = gate_weight.shape[1]
    chunk = d // gw
    capl = -(-cap // 128) * 128
    packed = chunk % 256 == 0
    own_shape = (n, PAIR, chunk // 2) if packed else (n, SLOT, chunk)
    own_type = BF16 if packed else F32
    vmem = pl.BlockSpec(memory_space=pltpu.VMEM)
    hbm = pl.BlockSpec(memory_space=pl.ANY)
    dma = pltpu.SemaphoreType.DMA
    value, grad, spread, gg = pl.pallas_call(
        functools.partial(kernel, n, experts, packed),
        out_shape=(
            jax.ShapeDtypeStruct((experts * SLOT, d), BF16),
            jax.ShapeDtypeStruct((experts * SLOT, d), BF16),
            jax.ShapeDtypeStruct((tok, experts * SLOT), BF16),
            jax.ShapeDtypeStruct((experts, cap), F32),
        ),
        in_specs=[hbm] * 5 + [vmem, pl.BlockSpec(memory_space=pltpu.SMEM), vmem],
        out_specs=(vmem, vmem, vmem, vmem),
        scratch_shapes=[
            pltpu.VMEM((tok, d), BF16),
            pltpu.VMEM((tok, d), BF16),
            pltpu.VMEM((gw, chunk, ff), BF16),
            pltpu.VMEM((gw, chunk, ff), BF16),
            pltpu.VMEM((gw, ff, chunk), BF16),
            pltpu.VMEM((n, PAIR, chunk), BF16),
            pltpu.VMEM((n, PAIR, chunk), BF16),
            pltpu.VMEM((gw, cap, chunk), BF16),
            pltpu.VMEM((gw, cap, chunk), BF16),
            pltpu.VMEM((cap, ff), F32),
            pltpu.VMEM((cap, ff), F32),
            pltpu.VMEM((cap, ff), F32),
            pltpu.VMEM((cap, chunk), F32),
            pltpu.VMEM((gw, cap, chunk), BF16),
            pltpu.VMEM((gw, cap, chunk), BF16),
            pltpu.VMEM((gw // 2, cap, chunk), BF16),
            pltpu.VMEM((gw // 2, cap, chunk), BF16),
            pltpu.VMEM((gw // 2, cap, chunk), BF16),
            pltpu.VMEM((gw // 2, cap, chunk), BF16),
            pltpu.VMEM(own_shape, own_type),
            pltpu.VMEM(own_shape, own_type),
            pltpu.VMEM(own_shape, own_type),
            pltpu.VMEM(own_shape, own_type),
            pltpu.VMEM((8, capl), F32),
            pltpu.VMEM((n, 8, capl), F32),
            dma((2,)), dma((gw,)), dma((gw,)), dma((gw,)),
            dma((n,)), dma((n,)),
            dma((gw,)), dma((gw,)), dma((gw,)), dma((gw,)),
            dma((gw,)), dma((gw // 2,)), dma((gw // 2,)), dma((gw,)), dma((gw // 2,)), dma((gw // 2,)),
            dma((n,)), dma((n,)), dma((n,)), dma((n,)), dma((n,)), dma((n,)),
        ],
        compiler_params=pltpu.CompilerParams(
            collective_id=0, has_side_effects=True, vmem_limit_bytes=56 * 1024 * 1024
        ),
        name="expert_layer",
    )(tokens, cotangent, gate_weight, up_weight, down_weight, chosen, counts, gate_values)
    steps = 4
    part = d // steps
    whole = pl.BlockSpec((tok, experts * SLOT), lambda i: (0, 0))
    rows = pl.BlockSpec((experts * SLOT, part), lambda i: (0, i))
    wide = pl.BlockSpec((tok, part), lambda i: (0, i))
    small = pl.BlockSpec((experts, cap), lambda i: (0, 0))
    return pl.pallas_call(
        expand,
        grid=(steps,),
        out_shape=(
            jax.ShapeDtypeStruct((tok, d), BF16),
            jax.ShapeDtypeStruct((tok, d), BF16),
            jax.ShapeDtypeStruct((experts, cap), F32),
        ),
        in_specs=[whole, rows, rows, small],
        out_specs=(wide, wide, small),
        name="expand_rows",
    )(spread, value, grad, gg)


def solution(mesh):
    placed = (
        P(("groups", "expert"), None),
        P(("groups", "expert"), None),
        P(None, "expert"),
        P(None, "expert"),
        P("expert", None),
        P("groups", None),
        P("groups"),
        P("groups", None),
    )
    return jax.shard_map(
        shards,
        mesh=mesh,
        in_specs=placed,
        out_specs=(P(("groups", "expert"), None), P(("groups", "expert"), None), P("groups", None)),
        check_vma=False,
    )
```

```python
import functools

import jax
import jax.numpy as jnp
from jax import lax
from jax.experimental import pallas as pl
from jax.experimental.pallas import tpu as pltpu
from jax.sharding import PartitionSpec as P

SLOT = 8
PAIR = 2 * SLOT
FAR = 1e9
F32 = jnp.float32
BF16 = jnp.bfloat16


def dot(a, b):
    return jnp.dot(a, b, preferred_element_type=F32)


def dot_nt(a, b):
    return lax.dot_general(a, b, (((1,), (1,)), ((), ())), preferred_element_type=F32)


def iota(shape, axis):
    return lax.broadcasted_iota(jnp.int32, shape, axis)


def hot(mask):
    return jnp.where(mask, 1.0, 0.0).astype(F32)


def kernel(
    n, experts, packed,
    tok_hbm, cot_hbm, wg_hbm, wu_hbm, wd_hbm, chosen_ref, counts_ref, gate_ref,
    out_ref, grad_ref, spread_ref, gg_ref,
    tok_v, cot_v, wg_v, wu_v, wd_v, send_a, land_a, rows_t, rows_g, acc_g, acc_u, acc_b, gg_acc,
    rs_send_v, rs_send_g, sib_v, sib_g, rs_v, rs_g, own_send_v, own_send_g, own_v, own_g, gg_send, gg_land,
    loc_sem, wg_sem, wu_sem, wd_sem,
    a_ss, a_rs, bt_ss, bt_rs, bg_ss, bg_rs, rv_ss, sv_rs, rv_rs, rg_ss, sg_rs, rg_rs, ov_ss, ov_rs, og_ss, og_rs, q_ss, q_rs,
):
    gw = n // experts
    me = lax.axis_index("expert")
    my_e = me // gw
    my_c = me % gw
    chips = gw // 2
    my_chip = my_c // 2
    core = my_c % 2
    sib = my_chip * 2 + 1 - core
    base = my_e * gw
    tok = tok_v.shape[0]
    chunk = rows_t.shape[2]
    cap = rows_t.shape[1]
    capl = gg_send.shape[1]
    flat = chips <= 4

    def other(i):
        return lax.rem(me + i, n)

    def back(i):
        return lax.rem(me + n - i, n)

    def ring(i):
        return lax.rem(my_c + i, gw)

    def ring_back(i):
        return lax.rem(my_c + gw - i, gw)

    def near(i):
        return lax.rem(my_chip + i, chips) * 2 + core

    def near_back(i):
        return lax.rem(my_chip + chips - i, chips) * 2 + core

    def twin(c):
        return c + 1 - 2 * core

    def remote(src, dst, ss, rs, to):
        return pltpu.make_async_remote_copy(
            src_ref=src, dst_ref=dst, send_sem=ss, recv_sem=rs,
            device_id={"expert": to}, device_id_type=pl.DeviceIdType.MESH,
        )

    tok_copy = pltpu.make_async_copy(tok_hbm, tok_v, loc_sem.at[0])
    cot_copy = pltpu.make_async_copy(cot_hbm, cot_v, loc_sem.at[1])
    tok_copy.start()
    cot_copy.start()

    def wg_copy(c):
        at = pl.multiple_of(c * chunk, chunk)
        return pltpu.make_async_copy(wg_hbm.at[pl.ds(at, chunk), :], wg_v.at[c], wg_sem.at[c])

    def wu_copy(c):
        at = pl.multiple_of(c * chunk, chunk)
        return pltpu.make_async_copy(wu_hbm.at[pl.ds(at, chunk), :], wu_v.at[c], wu_sem.at[c])

    def wd_copy(c):
        at = pl.multiple_of(c * chunk, chunk)
        return pltpu.make_async_copy(wd_hbm.at[:, pl.ds(at, chunk)], wd_v.at[c], wd_sem.at[c])

    barrier = pltpu.get_barrier_semaphore()

    @pl.loop(1, n)
    def _(i):
        pl.semaphore_signal(barrier, inc=1, device_id={"expert": other(i)}, device_id_type=pl.DeviceIdType.MESH)

    @pl.loop(0, gw)
    def _(i):
        c = ring_back(i)
        wg_copy(c).start()
        wu_copy(c).start()

    @pl.loop(0, gw)
    def _(i):
        wd_copy(ring(i)).start()

    k_row = iota((1, cap), 1)
    eye = iota((cap, cap), 0) == iota((cap, cap), 1)

    def table(e):
        row = jnp.where(k_row < counts_ref[e], chosen_ref[pl.ds(e, 1), :].astype(F32), FAR)
        col = jnp.sum(jnp.where(eye, row, 0.0), axis=1, keepdims=True)
        return row, col

    first = (me * tok).astype(F32)
    span = float(tok)
    pick = jnp.zeros((experts * SLOT, tok), F32)
    for e in range(experts):
        row, col = table(e)
        start = jnp.sum(hot(row < first), axis=1, keepdims=True)
        j_col = iota((experts * SLOT, cap), 0) - e * SLOT
        a = hot((iota((experts * SLOT, cap), 1).astype(F32) == start + j_col.astype(F32)) & (j_col >= 0) & (j_col < SLOT))
        b = hot(col == first + iota((cap, tok), 1).astype(F32))
        pick = pick + dot(a.astype(BF16), b.astype(BF16))
    pick = pick.astype(BF16)

    tok_copy.wait()
    cot_copy.wait()

    @pl.loop(0, gw, unroll=flat)
    def _(c):
        cols = pl.ds(pl.multiple_of(c * chunk, chunk), chunk)
        t = dot(pick, tok_v[:, cols])
        g = dot(pick, cot_v[:, cols])
        for e in range(experts):
            lo = e * SLOT
            send_a[e * gw + c] = jnp.concatenate([t[lo:lo + SLOT], g[lo:lo + SLOT]], axis=0).astype(BF16)

    pl.semaphore_wait(barrier, n - 1)

    def a_copy(to, slot_of):
        return remote(send_a.at[to], land_a.at[slot_of], a_ss.at[to], a_rs.at[slot_of], to)

    @pl.loop(1, n)
    def _(i):
        a_copy(other(i), me).start()

    land_a[me] = send_a[me]

    row, col = table(my_e)
    j = iota((cap, n * PAIR), 1)
    dev = (j // PAIR).astype(F32) * span
    slot = j % PAIR
    start = jnp.sum(hot(col < dev), axis=0, keepdims=True)
    inside = col < dev + span
    k_col = iota((cap, n * PAIR), 0).astype(F32)
    from_t = hot(inside & (slot < SLOT) & (k_col == start + slot.astype(F32))).astype(BF16)
    from_g = hot(inside & (slot >= SLOT) & (k_col == start + (slot - SLOT).astype(F32))).astype(BF16)
    j8 = iota((n * SLOT, cap), 0)
    dev8 = (j8 // SLOT).astype(F32) * span
    start8 = jnp.sum(hot(row < dev8), axis=1, keepdims=True)
    to_slot = hot(
        (row < dev8 + span) & (iota((n * SLOT, cap), 1).astype(F32) == start8 + (j8 % SLOT).astype(F32))
    ).astype(BF16)
    weight_row = jnp.where(k_row < counts_ref[my_e], gate_ref[pl.ds(my_e, 1), :], 0.0)
    weight = jnp.sum(jnp.where(eye, weight_row, 0.0), axis=1, keepdims=True)
    live_row = k_row < counts_ref[my_e]
    live = jnp.sum(jnp.where(eye, hot(live_row), 0.0), axis=1, keepdims=True)
    spread = jnp.zeros((tok, experts * SLOT), F32)
    for e in range(experts):
        row, _ = table(e)
        start = jnp.sum(hot(row < first), axis=1, keepdims=True)
        j_row = iota((cap, experts * SLOT), 1) - e * SLOT
        at = hot((iota((cap, experts * SLOT), 0).astype(F32) == start + j_row.astype(F32)) & (j_row >= 0) & (j_row < SLOT))
        bt = hot(row == first + iota((tok, cap), 0).astype(F32))
        spread = spread + dot(bt.astype(BF16), at.astype(BF16))
    spread_ref[...] = spread.astype(BF16)

    @pl.loop(1, n)
    def _(i):
        a_copy(me, back(i)).wait_recv()

    arrived = land_a[...].reshape(n * PAIR, chunk)
    rows_t[my_c] = dot(from_t, arrived).astype(BF16)

    def bt_copy(to, at, sem):
        return remote(rows_t.at[at], rows_t.at[at], bt_ss.at[sem], bt_rs.at[at], base + to)

    def bg_copy(to, at, sem):
        return remote(rows_g.at[at], rows_g.at[at], bg_ss.at[sem], bg_rs.at[at], base + to)

    @pl.loop(1, chips, unroll=flat)
    def _(i):
        c = near(i)
        bt_copy(c, my_c, c).start()

    bt_copy(sib, my_c, sib).start()
    rows_g[my_c] = dot(from_g, arrived).astype(BF16)

    @pl.loop(1, chips, unroll=flat)
    def _(i):
        c = near(i)
        bg_copy(c, my_c, c).start()

    bg_copy(sib, my_c, sib).start()

    def gate_up(c):
        wg_copy(c).wait()
        wu_copy(c).wait()
        x = rows_t[c]
        acc_g[...] += dot(x, wg_v[c])
        acc_u[...] += dot(x, wu_v[c])

    acc_g[...] = jnp.zeros_like(acc_g)
    acc_u[...] = jnp.zeros_like(acc_u)
    gate_up(my_c)
    bt_copy(my_c, sib, sib).wait_recv()
    gate_up(sib)

    @pl.loop(1, chips, unroll=flat)
    def _(i):
        c = near_back(i)
        bt_copy(my_c, c, c).wait_recv()
        bt_copy(sib, c, twin(c)).start()
        gate_up(c)

    @pl.loop(1, chips, unroll=flat)
    def _(i):
        c = near_back(i)
        bg_copy(my_c, c, c).wait_recv()
        bg_copy(sib, c, twin(c)).start()
        bt_copy(my_c, twin(c), c).wait_recv()
        gate_up(twin(c))

    pre_gate = acc_g[...]
    hidden = (pre_gate * jax.nn.sigmoid(pre_gate) * acc_u[...]).astype(BF16)

    def sv_copy(c, at):
        return remote(rs_send_v.at[c], sib_v.at[at], rv_ss.at[c], sv_rs.at[at], base + sib)

    def rv_copy(to, at):
        return remote(rs_send_v.at[to], rs_v.at[at], rv_ss.at[to], rv_rs.at[at], base + to)

    def sg_copy(c, at):
        return remote(rs_send_g.at[c], sib_g.at[at], rg_ss.at[c], sg_rs.at[at], base + sib)

    def rg_copy(to, at):
        return remote(rs_send_g.at[to], rs_g.at[at], rg_ss.at[to], rg_rs.at[at], base + to)

    gg_acc[...] = jnp.zeros_like(gg_acc)

    @pl.loop(1, chips + 1, unroll=flat)
    def _(i):
        c = twin(near(i))
        bg_copy(my_c, c, c).wait_recv()
        wd_copy(c).wait()
        value = dot(hidden, wd_v[c])
        rs_send_v[c] = value.astype(BF16)
        sv_copy(c, c // 2).start()
        gg_acc[...] += value * rows_g[c].astype(F32)

    @pl.loop(1, chips, unroll=flat)
    def _(i):
        c = near(i)
        wd_copy(c).wait()
        value = dot(hidden, wd_v[c])
        gg_acc[...] += value * rows_g[c].astype(F32)
        sv_copy(c, c // 2).wait_recv()
        rs_send_v[c] = (value + sib_v[c // 2].astype(F32)).astype(BF16)
        rv_copy(c, my_chip).start()

    wd_copy(my_c).wait()
    value = dot(hidden, wd_v[my_c])
    sv_copy(my_c, my_chip).wait_recv()
    rs_v[my_chip] = (value + sib_v[my_chip].astype(F32)).astype(BF16)
    terms = live * jnp.sum(gg_acc[...] + value * rows_g[my_c].astype(F32), axis=1, keepdims=True)
    wide = iota((cap, capl), 0) == iota((cap, capl), 1)
    gg_send[...] = jnp.broadcast_to(jnp.sum(jnp.where(wide, terms, 0.0), axis=0, keepdims=True), gg_send.shape)

    def q_copy(to, at):
        return remote(gg_send, gg_land.at[at], q_ss.at[to], q_rs.at[at], to)

    acc_b[...] = jnp.zeros_like(acc_b)

    def back_part(c):
        scaled = (weight * rows_g[c].astype(F32)).astype(BF16)
        return dot_nt(scaled, wd_v[c])

    @pl.loop(0, chips, unroll=flat)
    def _(p):
        acc_b[...] += back_part(2 * p) + back_part(2 * p + 1)

    up = acc_u[...]
    sig = jax.nn.sigmoid(pre_gate)
    backed = acc_b[...]
    d_gate = (backed * up * sig * (1.0 + pre_gate * (1.0 - sig))).astype(BF16)
    d_up = (backed * (pre_gate * sig)).astype(BF16)

    def to_owners(term, buf):
        slots = dot(to_slot, term.astype(BF16)).reshape(n, SLOT, chunk)
        if packed:
            half = chunk // 2
            slots = jnp.concatenate([slots[:, :, :half], slots[:, :, half:]], axis=1).astype(BF16)
        buf[...] = slots

    def summed(buf):
        return lax.fori_loop(1, chips, lambda c, s: s + buf[c].astype(F32), buf[0].astype(F32), unroll=flat)

    def ov_copy(to, at):
        return remote(own_send_v.at[to], own_v.at[at], ov_ss.at[to], ov_rs.at[at], to)

    def og_copy(to, at):
        return remote(own_send_g.at[to], own_g.at[at], og_ss.at[to], og_rs.at[at], to)

    def token_part(c):
        return dot_nt(d_gate, wg_v[c]) + dot_nt(d_up, wu_v[c])

    @pl.loop(1, chips + 1, unroll=flat)
    def _(i):
        c = twin(near(i))
        rs_send_g[c] = token_part(c).astype(BF16)
        sg_copy(c, c // 2).start()

    @pl.loop(1, chips, unroll=flat)
    def _(i):
        c = near(i)
        part = token_part(c)
        sg_copy(c, c // 2).wait_recv()
        rs_send_g[c] = (part + sib_g[c // 2].astype(F32)).astype(BF16)
        rg_copy(c, my_chip).start()

    part = token_part(my_c)
    sg_copy(my_c, my_chip).wait_recv()
    rs_g[my_chip] = (part + sib_g[my_chip].astype(F32)).astype(BF16)

    @pl.loop(1, chips, unroll=flat)
    def _(i):
        rv_copy(my_c, near_back(i) // 2).wait_recv()

    to_owners(weight * summed(rs_v), own_send_v)

    @pl.loop(1, n)
    def _(i):
        ov_copy(other(i), me).start()

    own_v[me] = own_send_v[me]

    @pl.loop(1, n)
    def _(i):
        q_copy(other(i), me).start()

    gg_land[me] = gg_send[...]

    @pl.loop(1, chips, unroll=flat)
    def _(i):
        rg_copy(my_c, near_back(i) // 2).wait_recv()

    to_owners(summed(rs_g), own_send_g)

    @pl.loop(1, n)
    def _(i):
        og_copy(other(i), me).start()

    own_g[me] = own_send_g[me]

    def unpack(x):
        x = x.astype(F32)
        if packed:
            x = jnp.concatenate([x[:SLOT], x[SLOT:]], axis=1)
        return x

    def finish(buf, ref):
        @pl.loop(0, gw, unroll=flat)
        def _(c):
            rows = jnp.concatenate([unpack(buf[e * gw + c]) for e in range(experts)], axis=0)
            cols = pl.ds(pl.multiple_of(c * chunk, chunk), chunk)
            ref[:, cols] = rows.astype(BF16)

    @pl.loop(1, n)
    def _(i):
        ov_copy(me, back(i)).wait_recv()

    finish(own_v, out_ref)

    @pl.loop(1, n)
    def _(i):
        q_copy(me, back(i)).wait_recv()

    for e in range(experts):
        total = lax.fori_loop(1, gw, lambda c, s: s + gg_land[e * gw + c], gg_land[e * gw])
        gg_ref[e:e + 1, :] = total[0:1, :cap]

    @pl.loop(1, n)
    def _(i):
        og_copy(me, back(i)).wait_recv()

    finish(own_g, grad_ref)

    @pl.loop(1, n)
    def _(i):
        to = other(i)
        a_copy(to, me).wait_send()
        q_copy(to, me).wait_send()
        ov_copy(to, me).wait_send()
        og_copy(to, me).wait_send()

    @pl.loop(1, gw)
    def _(i):
        c = ring(i)
        bt_copy(c, my_c, c).wait_send()
        bg_copy(c, my_c, c).wait_send()
        rv_copy(c, my_chip).wait_send()
        rg_copy(c, my_chip).wait_send()


def expand(spread_ref, value_ref, grad_ref, gg_in, out_ref, tg_ref, gg_ref):
    spread = spread_ref[...]
    out_ref[...] = dot(spread, value_ref[...]).astype(BF16)
    tg_ref[...] = dot(spread, grad_ref[...]).astype(BF16)
    gg_ref[...] = gg_in[...]


def shards(tokens, cotangent, gate_weight, up_weight, down_weight, chosen, counts, gate_values):
    n = lax.axis_size("expert")
    experts, cap = chosen.shape
    gw = n // experts
    tok, d = tokens.shape
    ff = gate_weight.shape[1]
    chunk = d // gw
    capl = -(-cap // 128) * 128
    packed = chunk % 256 == 0
    own_shape = (n, PAIR, chunk // 2) if packed else (n, SLOT, chunk)
    own_type = BF16 if packed else F32
    vmem = pl.BlockSpec(memory_space=pltpu.VMEM)
    hbm = pl.BlockSpec(memory_space=pl.ANY)
    dma = pltpu.SemaphoreType.DMA
    value, grad, spread, gg = pl.pallas_call(
        functools.partial(kernel, n, experts, packed),
        out_shape=(
            jax.ShapeDtypeStruct((experts * SLOT, d), BF16),
            jax.ShapeDtypeStruct((experts * SLOT, d), BF16),
            jax.ShapeDtypeStruct((tok, experts * SLOT), BF16),
            jax.ShapeDtypeStruct((experts, cap), F32),
        ),
        in_specs=[hbm] * 5 + [vmem, pl.BlockSpec(memory_space=pltpu.SMEM), vmem],
        out_specs=(vmem, vmem, vmem, vmem),
        scratch_shapes=[
            pltpu.VMEM((tok, d), BF16),
            pltpu.VMEM((tok, d), BF16),
            pltpu.VMEM((gw, chunk, ff), BF16),
            pltpu.VMEM((gw, chunk, ff), BF16),
            pltpu.VMEM((gw, ff, chunk), BF16),
            pltpu.VMEM((n, PAIR, chunk), BF16),
            pltpu.VMEM((n, PAIR, chunk), BF16),
            pltpu.VMEM((gw, cap, chunk), BF16),
            pltpu.VMEM((gw, cap, chunk), BF16),
            pltpu.VMEM((cap, ff), F32),
            pltpu.VMEM((cap, ff), F32),
            pltpu.VMEM((cap, ff), F32),
            pltpu.VMEM((cap, chunk), F32),
            pltpu.VMEM((gw, cap, chunk), BF16),
            pltpu.VMEM((gw, cap, chunk), BF16),
            pltpu.VMEM((gw // 2, cap, chunk), BF16),
            pltpu.VMEM((gw // 2, cap, chunk), BF16),
            pltpu.VMEM((gw // 2, cap, chunk), BF16),
            pltpu.VMEM((gw // 2, cap, chunk), BF16),
            pltpu.VMEM(own_shape, own_type),
            pltpu.VMEM(own_shape, own_type),
            pltpu.VMEM(own_shape, own_type),
            pltpu.VMEM(own_shape, own_type),
            pltpu.VMEM((8, capl), F32),
            pltpu.VMEM((n, 8, capl), F32),
            dma((2,)), dma((gw,)), dma((gw,)), dma((gw,)),
            dma((n,)), dma((n,)),
            dma((gw,)), dma((gw,)), dma((gw,)), dma((gw,)),
            dma((gw,)), dma((gw // 2,)), dma((gw // 2,)), dma((gw,)), dma((gw // 2,)), dma((gw // 2,)),
            dma((n,)), dma((n,)), dma((n,)), dma((n,)), dma((n,)), dma((n,)),
        ],
        compiler_params=pltpu.CompilerParams(
            collective_id=0, has_side_effects=True, vmem_limit_bytes=56 * 1024 * 1024
        ),
        name="expert_layer",
    )(tokens, cotangent, gate_weight, up_weight, down_weight, chosen, counts, gate_values)
    steps = 2
    part = d // steps
    whole = pl.BlockSpec((tok, experts * SLOT), lambda i: (0, 0))
    rows = pl.BlockSpec((experts * SLOT, part), lambda i: (0, i))
    wide = pl.BlockSpec((tok, part), lambda i: (0, i))
    small = pl.BlockSpec((experts, cap), lambda i: (0, 0))
    return pl.pallas_call(
        expand,
        grid=(steps,),
        out_shape=(
            jax.ShapeDtypeStruct((tok, d), BF16),
            jax.ShapeDtypeStruct((tok, d), BF16),
            jax.ShapeDtypeStruct((experts, cap), F32),
        ),
        in_specs=[whole, rows, rows, small],
        out_specs=(wide, wide, small),
        name="expand_rows",
    )(spread, value, grad, gg)


def solution(mesh):
    placed = (
        P(("groups", "expert"), None),
        P(("groups", "expert"), None),
        P(None, "expert"),
        P(None, "expert"),
        P("expert", None),
        P("groups", None),
        P("groups"),
        P("groups", None),
    )
    return jax.shard_map(
        shards,
        mesh=mesh,
        in_specs=placed,
        out_specs=(P(("groups", "expert"), None), P(("groups", "expert"), None), P("groups", None)),
        check_vma=False,
    )
```
